32 devices in a mesh: dp: 8 (over y, x, core), tensor: 4 (over z).
Axes of the slice: x: 2, y: 2, z: 4, core: 2. Of those that a mesh axis runs over, the one named last changes fastest.
Arguments:
- tokens: bfloat16 [24576, 1024], P(('dp', 'tensor')), may hold values from -6 to 6
- positions: int32 [24576], P('dp'), may hold values from 0 to 4092, as said below
- first_gain: bfloat16 [1024], replicated, may hold values from 0.099609375 to 1.8984375
- w_query: bfloat16 [1024, 2048], P(None, 'tensor'), may hold values from -0.1875 to 0.1875
- key_matrix: bfloat16 [1024, 1024], P(None, 'tensor'), may hold values from -0.1875 to 0.1875
- value_matrix: bfloat16 [1024, 1024], P(None, 'tensor'), may hold values from -0.1875 to 0.1875
- query_gain: bfloat16 [128], replicated, may hold values from 0.099609375 to 1.8984375
- key_gain: bfloat16 [128], replicated, may hold values from 0.099609375 to 1.8984375
- w_output: bfloat16 [2048, 1024], P('tensor'), may hold values from -0.5 to 0.5
- second_gain: bfloat16 [1024], replicated, may hold values from 0.099609375 to 1.8984375
- w_gate: bfloat16 [1024, 3072], P(None, 'tensor'), may hold values from -0.1875 to 0.1875
- w_up: bfloat16 [1024, 3072], P(None, 'tensor'), may hold values from -0.1875 to 0.1875
- w_down: bfloat16 [3072, 1024], P('tensor'), may hold values from -0.109375 to 0.109375
- out_grad: bfloat16 [24576, 1024], P(('dp', 'tensor')), may hold values from -6 to 6
Outputs:
- layer_out: bfloat16 [24576, 1024], P(('dp', 'tensor'))
- input_grad: bfloat16 [24576, 1024], P(('dp', 'tensor'))
- first_gain_grad: float32 [1024], P('tensor')
- query_weight_grad: float32 [1024, 2048], P(None, 'tensor')
- key_weight_grad: float32 [1024, 1024], P(None, 'tensor')
- value_weight_grad: float32 [1024, 1024], P(None, 'tensor')
- query_gain_grad: float32 [128], P('tensor')
- key_gain_grad: float32 [128], P('tensor')
- output_weight_grad: float32 [2048, 1024], P('tensor')
- second_gain_grad: float32 [1024], P('tensor')
- gate_weight_grad: float32 [1024, 3072], P(None, 'tensor')
- up_weight_grad: float32 [1024, 3072], P(None, 'tensor')
- down_weight_grad: float32 [3072, 1024], P('tensor')
The draws below stay inside these ranges and needn't reach their ends.
Inputs may be any that keep to these rules, and one draw needn't show every extreme that they name: Within each aligned block of 1024 rows (one sequence) positions start at 0 and rise by 1 to 4 from one row to the next.
All inputs are finite; a program needn't handle non-finite values.
Results may differ from the reference program's by a relative error of at most 0.023.
Values may be sent and summed in bfloat16 or wider, within the bound.
A program may use at most 256 MiB of HBM per device.

```python
import math
import jax
import jax.numpy as jnp
from jax import lax

MODEL_WIDTH = 1024
QUERY_HEADS = 16
KEY_VALUE_HEADS = 8
HEAD_SIZE = 128
FF = 3072
SEQUENCE_TOKENS = 1024
SEQS = 24
TOKENS = 24576


def draw_positions(key, part):
    key = jax.random.fold_in(key, 11)
    stride_key = jax.random.fold_in(key, 1)
    pick_key = jax.random.fold_in(key, 2)
    strides = jax.random.randint(stride_key, (TOKENS // SEQUENCE_TOKENS, SEQUENCE_TOKENS), 1, 5)
    chosen = jax.random.randint(pick_key, (), 0, TOKENS // SEQUENCE_TOKENS)
    row = lax.broadcasted_iota(jnp.int32, (TOKENS // SEQUENCE_TOKENS, SEQUENCE_TOKENS), 0)
    column = lax.broadcasted_iota(jnp.int32, (TOKENS // SEQUENCE_TOKENS, SEQUENCE_TOKENS), 1)
    strides = jnp.where(row == chosen, 4, strides)
    strides = jnp.where(column == 0, 0, strides).astype(jnp.int32)
    return jnp.cumsum(strides, axis=1).astype(jnp.int32).reshape(TOKENS)


def block_levels(key, dims, cuts, smallest, top_value):
    loudness, own = 1.0, jax.random.fold_in(key, 6)
    for position, shards_of in cuts:
        heights = jnp.exp(jax.random.uniform(jax.random.fold_in(own, position), (shards_of,), jnp.float32, smallest / len(cuts), top_value / len(cuts)))
        loudness = loudness * jnp.repeat(heights, dims[position] // shards_of).reshape([-1 if axis == position else 1 for axis in range(len(dims))])
    return loudness


def bell_draw(key, extent, scale, most, cuts=(), held_as=jnp.bfloat16):
    entries = jax.random.normal(key, extent, jnp.float32) * scale
    if len(cuts) > 0:
        entries = block_levels(key, extent, cuts, -0.22, 0.18) * entries
    return jnp.clip(entries, min=-most, max=most).astype(held_as)


def setup_inputs(seed: int = 0) -> dict:
    key_of = jax.random.split(jax.random.key(seed), 15)
    return {
        "tokens": bell_draw(key_of[0], (TOKENS, MODEL_WIDTH), 1.0, 6.0, ((0, 32),)),
        "positions": draw_positions(jax.random.fold_in(key_of[14], 71), 0),
        "first_gain": jnp.clip(1.0 + 0.18 * jax.random.normal(key_of[2], (MODEL_WIDTH,), jnp.float32), 0.099609375, 1.8984375).astype(jnp.bfloat16),
        "w_query": bell_draw(key_of[3], (MODEL_WIDTH, QUERY_HEADS * HEAD_SIZE), MODEL_WIDTH ** -0.5, 0.1875, ((1, 4),)),
        "key_matrix": bell_draw(key_of[4], (MODEL_WIDTH, KEY_VALUE_HEADS * HEAD_SIZE), MODEL_WIDTH ** -0.5, 0.1875, ((1, 4),)),
        "value_matrix": bell_draw(key_of[5], (MODEL_WIDTH, KEY_VALUE_HEADS * HEAD_SIZE), MODEL_WIDTH ** -0.5, 0.1875, ((1, 4),)),
        "query_gain": jnp.clip(1.0 + 0.18 * jax.random.normal(key_of[6], (HEAD_SIZE,), jnp.float32), 0.099609375, 1.8984375).astype(jnp.bfloat16),
        "key_gain": jnp.clip(1.0 + 0.18 * jax.random.normal(key_of[7], (HEAD_SIZE,), jnp.float32), 0.099609375, 1.8984375).astype(jnp.bfloat16),
        "w_output": bell_draw(key_of[8], (QUERY_HEADS * HEAD_SIZE, MODEL_WIDTH), (QUERY_HEADS * HEAD_SIZE // 16) ** -0.5, 0.5, ((0, 4),)),
        "second_gain": jnp.clip(1.0 + 0.18 * jax.random.normal(key_of[9], (MODEL_WIDTH,), jnp.float32), 0.099609375, 1.8984375).astype(jnp.bfloat16),
        "w_gate": bell_draw(key_of[10], (MODEL_WIDTH, FF), MODEL_WIDTH ** -0.5, 0.1875, ((1, 4),)),
        "w_up": bell_draw(key_of[11], (MODEL_WIDTH, FF), MODEL_WIDTH ** -0.5, 0.1875, ((1, 4),)),
        "w_down": bell_draw(key_of[12], (FF, MODEL_WIDTH), FF ** -0.5, 0.109375, ((0, 4),)),
        "out_grad": bell_draw(key_of[13], (TOKENS, MODEL_WIDTH), 1.0, 6.0, ((0, 32),)),
    }


epsilon = 1e-06
rope_base = 1000000.0

@jax.custom_vjp
def lower_part(v):
    return lax.optimization_barrier(v.astype(jnp.bfloat16)).astype(jnp.float32)

@jax.custom_vjp
def lower_backward(v):
    return v

def low_keep(v):
    return (lower_part(v), None)

def low_pass(kept, grad):
    return (grad,)

def back_keep(v):
    return (v, None)

def back_low(kept, grad):
    return (lower_part(grad),)
lower_part.defvjp(low_keep, low_pass)
lower_backward.defvjp(back_keep, back_low)

def elementwise_product(left, right):
    return jnp.dot(left, right, precision=lax.Precision.HIGHEST, preferred_element_type=jnp.float32)

def rms_scale(value, gain):
    return value * lax.rsqrt(lax.optimization_barrier(jnp.mean(value * value, axis=-1, keepdims=True)) + epsilon) * gain

def rotary(value, cosine, sine):
    half = value.shape[-1] // 2
    first = value[..., :half]
    second = value[..., half:]
    return jnp.concatenate([first * cosine - second * sine, second * cosine + first * sine], axis=-1)

def attend_block(q_blk, key_rows, value_rows, start):
    scores = jnp.einsum('qhd,khd->hqk', q_blk, key_rows, precision=lax.Precision.HIGHEST) * HEAD_SIZE ** (-0.5)
    scores = lower_backward(scores)
    row_ids = start + lax.broadcasted_iota(jnp.int32, (q_blk.shape[0], key_rows.shape[0]), 0)
    col_ids = lax.broadcasted_iota(jnp.int32, (q_blk.shape[0], key_rows.shape[0]), 1)
    scores = jnp.where((col_ids <= row_ids)[None], scores, -1e+30)
    top = lax.optimization_barrier(jnp.max(scores, axis=-1, keepdims=True))
    expo = jnp.exp(scores - top)
    probs = lower_part(expo / lax.optimization_barrier(jnp.sum(expo, axis=-1, keepdims=True)))
    return jnp.einsum('hqk,khd->qhd', probs, value_rows, precision=lax.Precision.HIGHEST)

def attention(query, key_rows, value_rows):
    sequence_count = query.shape[0] // SEQUENCE_TOKENS
    block = min(512, SEQUENCE_TOKENS)
    query = query.reshape(sequence_count, SEQUENCE_TOKENS // block, block, QUERY_HEADS, HEAD_SIZE)
    key_rows = jnp.repeat(key_rows.reshape(sequence_count, SEQUENCE_TOKENS, KEY_VALUE_HEADS, HEAD_SIZE), QUERY_HEADS // KEY_VALUE_HEADS, axis=2)
    value_rows = jnp.repeat(value_rows.reshape(sequence_count, SEQUENCE_TOKENS, KEY_VALUE_HEADS, HEAD_SIZE), QUERY_HEADS // KEY_VALUE_HEADS, axis=2)
    starts = jnp.arange(SEQUENCE_TOKENS // block, dtype=jnp.int32) * block

    def one_seq(item):
        q_seq, k_seq, v_seq = item

        def one_block(pair):
            return attend_block(pair[0], k_seq, v_seq, pair[1])
        return lax.map(jax.checkpoint(one_block), (q_seq, starts))
    return lax.map(one_seq, (query, key_rows, value_rows)).reshape(sequence_count * SEQUENCE_TOKENS, QUERY_HEADS * HEAD_SIZE)

def layer(x, angle, first_gain, w_query, key_matrix, value_matrix, query_gain, key_gain, w_output, second_gain, w_gate, w_up, w_down):
    cosine = jnp.cos(angle)[:, None, :]
    sine = jnp.sin(angle)[:, None, :]
    hidden_first = lower_part(rms_scale(x, first_gain))
    q_raw = lower_backward(elementwise_product(hidden_first, w_query)).reshape(-1, QUERY_HEADS, HEAD_SIZE)
    key_unnormed = lower_backward(elementwise_product(hidden_first, key_matrix)).reshape(-1, KEY_VALUE_HEADS, HEAD_SIZE)
    value_rows = lower_part(lower_backward(elementwise_product(hidden_first, value_matrix))).reshape(-1, KEY_VALUE_HEADS, HEAD_SIZE)
    query = lower_part(rotary(rms_scale(q_raw, query_gain), cosine, sine))
    key_rows = lower_part(rotary(rms_scale(key_unnormed, key_gain), cosine, sine))
    heads = lower_part(lower_backward(attention(query, key_rows, value_rows)))
    x1 = x + lower_backward(elementwise_product(heads, w_output))
    h2 = lower_part(rms_scale(x1, second_gain))
    gate = lower_backward(elementwise_product(h2, w_gate))
    up_part = lower_backward(elementwise_product(h2, w_up))
    hidden = lower_part(gate * jax.nn.sigmoid(gate) * up_part)
    return x1 + lower_backward(elementwise_product(hidden, w_down))

def reference(tokens, positions, first_gain, w_query, key_matrix, value_matrix, query_gain, key_gain, w_output, second_gain, w_gate, w_up, w_down, out_grad):
    group = 1
    for count in range(1, SEQS + 1):
        if SEQS % count == 0 and count * SEQUENCE_TOKENS <= 4096:
            group = count
    turns = SEQS // group
    rate = jnp.exp(-math.log(rope_base) * 2.0 * jnp.arange(HEAD_SIZE // 2, dtype=jnp.float32) / HEAD_SIZE)
    angles = positions.astype(jnp.float32)[:, None] * rate[None, :]
    weights = tuple((w.astype(jnp.float32) for w in (first_gain, w_query, key_matrix, value_matrix, query_gain, key_gain, w_output, second_gain, w_gate, w_up, w_down)))
    inputs = tokens.astype(jnp.float32).reshape(turns, group * SEQUENCE_TOKENS, MODEL_WIDTH)
    cotangents = out_grad.astype(jnp.float32).reshape(turns, group * SEQUENCE_TOKENS, MODEL_WIDTH)
    angle_sets = angles.reshape(turns, group * SEQUENCE_TOKENS, HEAD_SIZE // 2)

    def step(acc, item):
        x, angle, cotangent = item
        result, pull = jax.vjp(lambda value, *params: layer(value, angle, *params), x, *weights)
        grads = pull(cotangent)
        acc = tuple((a + g for a, g in zip(acc, grads[1:])))
        return (acc, (result.astype(jnp.bfloat16), grads[0].astype(jnp.bfloat16)))
    start = tuple((jnp.zeros(w.shape, jnp.float32) for w in weights))
    acc, (results, in_grads) = lax.scan(step, start, (inputs, angle_sets, cotangents))
    return (results.reshape(TOKENS, MODEL_WIDTH), in_grads.reshape(TOKENS, MODEL_WIDTH), acc[0], acc[1], acc[2], acc[3], acc[4], acc[5], acc[6], acc[7], acc[8], acc[9], acc[10])
```

```python
import functools
import math

import jax
import jax.numpy as jnp
from jax import lax
from jax.experimental import pallas as pl
from jax.experimental.pallas import tpu as pltpu
from jax.sharding import Mesh, PartitionSpec as P

SEQUENCE_TOKENS = 1024
HEAD = 128
epsilon = 1e-06
rope_base = 1000000.0
BF = jnp.bfloat16
F32 = jnp.float32
MIB = 1024 * 1024


def norm_forward(value, gain):
    inverse = lax.rsqrt(jnp.mean(value * value, axis=-1, keepdims=True) + epsilon)
    unit = value * inverse
    return (unit * gain, unit, inverse)


def norm_backward(grad, unit, inverse, gain):
    scaled = grad * gain
    back = inverse * (scaled - unit * jnp.mean(scaled * unit, axis=-1, keepdims=True))
    return back, grad * unit


def nn(left, right):
    return jnp.dot(left, right, preferred_element_type=F32)


def nt(left, right):
    return lax.dot_general(left, right, (((1,), (1,)), ((), ())), preferred_element_type=F32)


def tn(left, right):
    return lax.dot_general(left, right, (((0,), (0,)), ((), ())), preferred_element_type=F32)


def project(h_ref, w_ref, cos_ref, sin_ref, gq_ref, gk_ref, halo, qw):
    cos, sin = cos_ref[0], sin_ref[0]
    turn = lambda u, c, s: u * c + pltpu.roll(u, HEAD // 2, 1) * s
    kv = nn(h_ref[0], w_ref[0, :, qw:])
    kvw = kv.shape[1] // 2
    q_raw = nn(h_ref[0, halo:], w_ref[0, :, :qw])
    qs, ks = [], []
    for i in range(qw // HEAD):
        y, unit, inv = norm_forward(q_raw[:, i * HEAD : (i + 1) * HEAD], gq_ref[...])
        qs.append((turn(y, cos[halo:], sin[halo:]).astype(BF), unit, inv))
    for i in range(kvw // HEAD):
        y, unit, inv = norm_forward(kv[:, i * HEAD : (i + 1) * HEAD], gk_ref[...])
        v = kv[:, kvw + i * HEAD : kvw + (i + 1) * HEAD].astype(BF)
        ks.append((turn(y, cos, sin).astype(BF), unit, inv, v))
    return qs, ks


def attend_kernel(halo, block, qw, t_ref, h_ref, w_ref, cos_ref, sin_ref, gq_ref, gk_ref,
                  o_ref, l_ref, q_s, k_s, v_s, acc):
    qs, ks = project(h_ref, w_ref, cos_ref, sin_ref, gq_ref, gk_ref, halo, qw)
    rows = q_s.shape[0]
    group = len(qs) // len(ks)
    rate = HEAD**-0.5 * math.log2(math.e)
    whole = SEQUENCE_TOKENS // block
    first = t_ref[0] * (rows // block)
    low = lax.broadcasted_iota(jnp.int32, (block, block), 1) <= lax.broadcasted_iota(
        jnp.int32, (block, block), 0)
    for i, (q, _, _) in enumerate(qs):
        k, _, _, v = ks[i // group]
        q_s[...] = q
        if i % group == 0:
            k_s[...] = k
            v_s[...] = jnp.concatenate([v, jnp.ones_like(v)], axis=1)
        for b in range(rows // block):
            before = lax.rem(first + b, whole)
            qb = q_s[b * block : (b + 1) * block]
            own = halo + b * block
            s = nt(qb, k_s[own : own + block])
            e = jnp.where(low, jnp.exp2(s * rate), 0.0).astype(BF)
            acc[...] = nn(e, v_s[own : own + block])
            for j in range(1, whole):
                at = own - j * block
                if at < 0:
                    break

                @pl.when(before >= j)
                def _():
                    e = jnp.exp2(nt(qb, k_s[at : at + block]) * rate).astype(BF)
                    acc[...] += nn(e, v_s[at : at + block])

            inv = 1.0 / acc[:, HEAD:]
            o_ref[0, b * block : (b + 1) * block, i * HEAD : (i + 1) * HEAD] = (
                acc[:, :HEAD] * inv).astype(BF)
            l_ref[0, b * block : (b + 1) * block, i * HEAD : (i + 1) * HEAD] = inv


def attend_back_kernel(halo, block, qw, t_ref, h_ref, w_ref, cos_ref, sin_ref, gq_ref, gk_ref,
                       o_ref, l_ref, da_ref, wo_ref,
                       dq_ref, dkv_ref, share_ref, q_s, k_s, v_s, d_s, dq_s, dk_s, dv_s):
    qs, ks = project(h_ref, w_ref, cos_ref, sin_ref, gq_ref, gk_ref, halo, qw)
    rows, keys = q_s.shape[0], k_s.shape[0]
    group = len(qs) // len(ks)
    scale = HEAD**-0.5
    rate = scale * math.log2(math.e)
    whole = SEQUENCE_TOKENS // block
    first = t_ref[0] * (rows // block)
    high = lax.broadcasted_iota(jnp.int32, (block, block), 0) <= lax.broadcasted_iota(
        jnp.int32, (block, block), 1)
    cos, sin = cos_ref[0], sin_ref[0]
    back_turn = lambda g, c, s: g * c - pltpu.roll(g, HEAD // 2, 1) * s
    do = nt(da_ref[0], wo_ref[0]).astype(BF)
    kvw = len(ks) * HEAD
    share_q = jnp.zeros((1, HEAD), F32)
    share_k = jnp.zeros((1, HEAD), F32)
    for i, (q, unit_q, inv_q) in enumerate(qs):
        k, unit_k, inv_k, v = ks[i // group]
        at_head = slice(i * HEAD, (i + 1) * HEAD)
        q_s[...] = q
        if i % group == 0:
            k_s[...] = k
            lane = lax.broadcasted_iota(jnp.int32, (keys, HEAD), 1)
            v_s[...] = jnp.concatenate([v, jnp.where(lane < 2, 1.0, 0.0).astype(BF)], axis=1)
            dk_s[...] = jnp.zeros_like(dk_s)
            dv_s[...] = jnp.zeros_like(dv_s)
        d = (do[:, at_head].astype(F32) * l_ref[0, :, at_head]).astype(BF)
        delta = jnp.sum(d.astype(F32) * o_ref[0, :, at_head].astype(F32), axis=1, keepdims=True)
        upper = delta.astype(BF).astype(F32)
        lane = lax.broadcasted_iota(jnp.int32, (rows, HEAD), 1)
        extra = jnp.where(lane == 0, -upper, jnp.where(lane == 1, upper - delta, 0.0))
        d_s[...] = jnp.concatenate([d, extra.astype(BF)], axis=1)
        for b in range(rows // block):
            before = lax.rem(first + b, whole)
            qr = slice(b * block, (b + 1) * block)
            own = halo + b * block

            def part(at, masked):
                kr = slice(at, at + block)
                e = jnp.exp2(nt(k_s[kr], q_s[qr]) * rate)
                if masked:
                    e = jnp.where(high, e, 0.0)
                ds = (e * nt(v_s[kr], d_s[qr])).astype(BF)
                dv_s[kr] += nn(e.astype(BF), d_s[qr, :HEAD])
                dk_s[kr] += nn(ds, q_s[qr])
                return tn(ds, k_s[kr])

            dq_s[qr] = part(own, True)
            for j in range(1, whole):
                at = own - j * block
                if at < 0:
                    break

                @pl.when(before >= j)
                def _():
                    dq_s[qr] += part(at, False)

        grad = back_turn(dq_s[...] * scale, cos[halo:], sin[halo:])
        back, share = norm_backward(grad, unit_q, inv_q, gq_ref[...])
        share_q += jnp.sum(share, axis=0, keepdims=True)
        dq_ref[0, 0, :, at_head] = back.astype(BF)
        if i % group == group - 1:
            kh = i // group
            grad = back_turn(dk_s[...] * scale, cos, sin)
            back, share = norm_backward(grad, unit_k, inv_k, gk_ref[...])
            share_k += jnp.sum(share, axis=0, keepdims=True)
            dkv_ref[0, 0, :, kh * HEAD : (kh + 1) * HEAD] = back.astype(BF)
            dkv_ref[0, 0, :, kvw + kh * HEAD : kvw + (kh + 1) * HEAD] = dv_s[...].astype(BF)
    share_ref[0, 0] = jnp.concatenate(
        [share_q, share_k, jnp.zeros((6, HEAD), F32)], axis=0)


def attention_specs(keys, width, qkv, tensor):
    return [
        pl.BlockSpec(memory_space=pltpu.SMEM),
        pl.BlockSpec((1, keys, width), lambda s, t: (s, 0, 0)),
        pl.BlockSpec((1, width, qkv), lambda s, t: (t, 0, 0)),
        pl.BlockSpec((1, keys, HEAD), lambda s, t: (s, 0, 0)),
        pl.BlockSpec((1, keys, HEAD), lambda s, t: (s, 0, 0)),
        pl.BlockSpec((1, HEAD), lambda s, t: (0, 0)),
        pl.BlockSpec((1, HEAD), lambda s, t: (0, 0)),
    ]


def attend(block, halo, qw, t, h1, wqkv, cos, sin, gq, gk):
    split, keys, width = h1.shape
    tensor, _, qkv = wqkv.shape
    rows = keys - halo
    head_block = pl.BlockSpec((1, rows, qw), lambda s, t: (s, 0, t))
    return pl.pallas_call(
        functools.partial(attend_kernel, halo, block, qw),
        grid=(split, tensor),
        in_specs=attention_specs(keys, width, qkv, tensor),
        out_specs=[head_block, head_block],
        out_shape=[
            jax.ShapeDtypeStruct((split, rows, tensor * qw), BF),
            jax.ShapeDtypeStruct((split, rows, tensor * qw), F32),
        ],
        scratch_shapes=[
            pltpu.VMEM((rows, HEAD), BF),
            pltpu.VMEM((keys, HEAD), BF),
            pltpu.VMEM((keys, 2 * HEAD), BF),
            pltpu.VMEM((block, 2 * HEAD), F32),
        ],
        cost_estimate=pl.CostEstimate(
            flops=60_000_000_000, bytes_accessed=30_000_000, transcendentals=10_000_000),
        compiler_params=pltpu.CompilerParams(vmem_limit_bytes=48 * MIB),
    )(t, h1, wqkv, cos, sin, gq, gk)


def attend_back(block, halo, qw, t, h1, wqkv, cos, sin, gq, gk, o, l, da, wo):
    split, keys, width = h1.shape
    tensor, _, qkv = wqkv.shape
    rows = keys - halo
    head_block = pl.BlockSpec((1, rows, qw), lambda s, t: (s, 0, t))
    return pl.pallas_call(
        functools.partial(attend_back_kernel, halo, block, qw),
        grid=(split, tensor),
        in_specs=attention_specs(keys, width, qkv, tensor)
        + [
            head_block,
            head_block,
            pl.BlockSpec((1, rows, width), lambda s, t: (s, 0, 0)),
            pl.BlockSpec((1, qw, width), lambda s, t: (t, 0, 0)),
        ],
        out_specs=[
            pl.BlockSpec((1, 1, rows, qw), lambda s, t: (t, s, 0, 0)),
            pl.BlockSpec((1, 1, keys, qkv - qw), lambda s, t: (t, s, 0, 0)),
            pl.BlockSpec((1, 1, 8, HEAD), lambda s, t: (t, s, 0, 0)),
        ],
        out_shape=[
            jax.ShapeDtypeStruct((tensor, split, rows, qw), BF),
            jax.ShapeDtypeStruct((tensor, split, keys, qkv - qw), BF),
            jax.ShapeDtypeStruct((tensor, split, 8, HEAD), F32),
        ],
        scratch_shapes=[
            pltpu.VMEM((rows, HEAD), BF),
            pltpu.VMEM((keys, HEAD), BF),
            pltpu.VMEM((keys, 2 * HEAD), BF),
            pltpu.VMEM((rows, 2 * HEAD), BF),
            pltpu.VMEM((rows, HEAD), F32),
            pltpu.VMEM((keys, HEAD), F32),
            pltpu.VMEM((keys, HEAD), F32),
        ],
        cost_estimate=pl.CostEstimate(
            flops=120_000_000_000, bytes_accessed=40_000_000, transcendentals=10_000_000),
        compiler_params=pltpu.CompilerParams(vmem_limit_bytes=56 * MIB),
    )(t, h1, wqkv, cos, sin, gq, gk, o, l, da, wo)


def feed_kernel(chunk, h_ref, ht_ref, dy_ref, wgu_ref, wd_ref,
                y_ref, dh_ref, dgu_ref, dwd_ref, hid_s, dg_s, du_s):
    rows = h_ref.shape[0]
    width = wd_ref.shape[1]

    @pl.when(pl.program_id(0) == 0)
    def _():
        y_ref[...] = jnp.zeros_like(y_ref)
        dh_ref[...] = jnp.zeros_like(dh_ref)

    for c in range(rows // chunk):
        at = slice(c * chunk, (c + 1) * chunk)
        gate = nn(h_ref[at], wgu_ref[0, :, :width])
        up = nn(h_ref[at], wgu_ref[0, :, width:])
        dhid = nt(dy_ref[at], wd_ref[0])
        sigma = 1.0 / (1.0 + jnp.exp(-gate))
        act = gate * sigma
        hid_s[at] = (act * up).astype(BF)
        du_s[at] = (dhid * act).astype(BF)
        dg_s[at] = (dhid * up * (sigma + act * (1.0 - sigma))).astype(BF)
        y_ref[at] += nn(hid_s[at], wd_ref[0])
        dh_ref[at] += nt(dg_s[at], wgu_ref[0, :, :width]) + nt(du_s[at], wgu_ref[0, :, width:])
    dgu_ref[0, :, :width] = nn(ht_ref[...], dg_s[...]).astype(BF)
    dgu_ref[0, :, width:] = nn(ht_ref[...], du_s[...]).astype(BF)
    dwd_ref[0] = tn(hid_s[...], dy_ref[...]).astype(BF)


def feed(h2, dy, wgu, wd):
    rows, model = h2.shape
    tensor, _, two = wgu.shape
    width = two // 2
    whole = pl.BlockSpec(memory_space=pltpu.VMEM)
    return pl.pallas_call(
        functools.partial(feed_kernel, rows // max(1, rows // 512)),
        grid=(tensor,),
        in_specs=[
            whole, whole, whole,
            pl.BlockSpec((1, model, two), lambda t: (t, 0, 0)),
            pl.BlockSpec((1, width, model), lambda t: (t, 0, 0)),
        ],
        out_specs=[
            whole, whole,
            pl.BlockSpec((1, model, two), lambda t: (t, 0, 0)),
            pl.BlockSpec((1, width, model), lambda t: (t, 0, 0)),
        ],
        out_shape=[
            jax.ShapeDtypeStruct((rows, model), F32),
            jax.ShapeDtypeStruct((rows, model), F32),
            jax.ShapeDtypeStruct((tensor, model, two), BF),
            jax.ShapeDtypeStruct((tensor, width, model), BF),
        ],
        scratch_shapes=[pltpu.VMEM((rows, width), BF)] * 3,
        cost_estimate=pl.CostEstimate(
            flops=50_000_000_000, bytes_accessed=40_000_000, transcendentals=3_000_000),
        compiler_params=pltpu.CompilerParams(vmem_limit_bytes=58 * MIB),
    )(h2, h2.T, dy, wgu, wd)


def on_device(pairs, split, tensor, tokens, positions, first_gain, w_query, key_matrix,
              value_matrix, query_gain, key_gain, w_output, second_gain, w_gate, w_up, w_down,
              out_grad):
    rows, model = tokens.shape
    pair, core, t = lax.axis_index("pair"), lax.axis_index("core"), lax.axis_index("tensor")
    hops = max(-(-(d * rows % SEQUENCE_TOKENS) // rows) for d in range(tensor))
    halo = hops * rows
    block = math.gcd(rows, 256)
    keys = halo + rows
    spread, home = ("tensor", "pair"), ("pair", "core")

    def other(value):
        return lax.ppermute(value, "core", [(0, 1), (1, 0)])

    def both(value):
        return jnp.stack([value, other(value)]) if split == 2 else value[None]

    def own_sum(parts):
        return parts[0] + other(parts[1].astype(BF)).astype(F32) if split == 2 else parts[0]

    def columns(w):
        cols, deep = w.shape[1] // split, w.shape[0] // pairs
        return lax.dynamic_slice(w, (pair * deep, core * cols), (deep, cols))

    def lines(w):
        deep = w.shape[0] // (split * pairs)
        return lax.dynamic_slice_in_dim(w, (core * pairs + pair) * deep, deep, 0)

    def gather(w):
        return lax.all_gather(w, spread, axis=0, tiled=True)

    reach = [
        lax.ppermute(tokens, "tensor", [(d, d + h) for d in range(tensor - h)])
        for h in range(hops, 0, -1)
    ]
    wqkv = gather(jnp.concatenate([columns(w_query), columns(key_matrix), columns(value_matrix)], 1))
    wqkv = wqkv.reshape(tensor, model, -1)
    qw = w_query.shape[1] // split
    wo = gather(lines(w_output)).reshape(tensor, qw, model)
    wgu = gather(jnp.concatenate([columns(w_gate), columns(w_up)], 1)).reshape(tensor, model, -1)
    wd = gather(lines(w_down)).reshape(tensor, -1, model)

    gain_one = first_gain.astype(F32)
    gain_two = second_gain.astype(F32)
    gq = query_gain.astype(F32)[None]
    gk = key_gain.astype(F32)[None]
    rate = jnp.exp(-math.log(rope_base) * 2.0 * jnp.arange(HEAD // 2, dtype=F32) / HEAD)
    place = jnp.concatenate([jnp.zeros((halo,), F32), positions.astype(F32)])
    place = both(lax.dynamic_slice_in_dim(place, t * rows, keys, 0))
    angles = place[..., None] * rate
    cosine, sine = jnp.cos(angles), jnp.sin(angles)
    cos = jnp.concatenate([cosine, cosine], axis=-1)
    sin = jnp.concatenate([-sine, sine], axis=-1)
    t_ref = t[None].astype(jnp.int32)

    resid = tokens.astype(F32)
    _, unit_one, inv_one = norm_forward(resid, gain_one)
    seen = both(jnp.concatenate(reach + [tokens], axis=0))
    h1 = norm_forward(seen.astype(F32), gain_one)[0].astype(BF)
    grads = both(out_grad)
    o, l = attend(block, halo, qw, t_ref, h1, wqkv, cos, sin, gq, gk)
    o_rows = o.reshape(split * rows, -1)
    wo_flat = wo.reshape(-1, model)
    mid = resid + own_sum(nn(o_rows, wo_flat).reshape(split, rows, model))
    normed_two, unit_two, inv_two = norm_forward(mid, gain_two)
    h2 = both(normed_two.astype(BF)).reshape(split * rows, model)
    y, dh2, dgu, dwd = feed(h2, grads.reshape(split * rows, model), wgu, wd)
    layer_out = (mid + own_sum(y.reshape(split, rows, model))).astype(BF)
    dh2 = own_sum(dh2.reshape(split, rows, model))
    back_two, share_two = norm_backward(dh2, unit_two, inv_two, gain_two)
    mid_grad = out_grad.astype(F32) + back_two
    da = both(mid_grad.astype(BF))
    dwo = tn(o_rows, da.reshape(split * rows, model)).astype(BF)
    dq, dkv, shares = attend_back(
        block, halo, qw, t_ref, h1, wqkv, cos, sin, gq, gk, o, l, da, wo)

    dh_kv = jnp.zeros((split * keys, model), F32)
    dh_q = jnp.zeros((split * rows, model), F32)
    h_rows = h1[:, halo:].reshape(split * rows, model)
    h_keys = h1.reshape(split * keys, model)
    terms = []
    for d in range(tensor):
        dq_d = dq[d].reshape(split * rows, -1)
        dkv_d = dkv[d].reshape(split * keys, -1)
        dh_kv += nt(dkv_d, wqkv[d, :, qw:])
        dh_q += nt(dq_d, wqkv[d, :, :qw])
        terms.append(jnp.concatenate([tn(h_rows, dq_d), tn(h_keys, dkv_d)], axis=1).astype(BF))
    dh_kv = dh_kv.reshape(split, keys, model)
    dh_own = own_sum(dh_kv[:, halo:] + dh_q.reshape(split, rows, model))
    if hops:
        dh_far = own_sum(dh_kv[:, :halo]).astype(BF)
        for h in range(hops, 0, -1):
            at = (hops - h) * rows
            dh_own += lax.ppermute(
                dh_far[at : at + rows], "tensor", [(d + h, d) for d in range(tensor - h)]
            ).astype(F32)
    back_one, share_one = norm_backward(dh_own, unit_one, inv_one, gain_one)
    input_grad = (mid_grad + back_one).astype(BF)

    def reduce(w):
        return lax.psum_scatter(w.reshape(-1, w.shape[-1]), spread, scatter_dimension=0, tiled=True)

    def from_columns(w):
        deep, cols = w.shape
        w = lax.all_gather(w, home, axis=0, tiled=True).reshape(pairs, split, deep, cols)
        return w

    def join(w, start, cols):
        w = w[..., start : start + cols]
        return w.transpose(0, 2, 1, 3).reshape(model, split * cols).astype(F32)

    def from_lines(w):
        return lax.all_gather(w, ("core", "pair"), axis=0, tiled=True).astype(F32)

    gu = from_columns(reduce(dgu))
    down_wgrad = from_lines(reduce(dwd))
    out_wgrad = from_lines(reduce(dwo))
    qkv = from_columns(reduce(jnp.stack(terms)))
    fw = gu.shape[-1] // 2
    kw = (qkv.shape[-1] - qw) // 2
    shares = jnp.sum(shares, axis=(0, 1))
    gains = jnp.concatenate(
        [jnp.sum(share_one, axis=0), jnp.sum(share_two, axis=0), shares[0], shares[1]])
    gains = lax.psum(gains, ("pair", "core", "tensor"))

    def piece(start, size):
        return lax.dynamic_slice_in_dim(gains, start + t * (size // tensor), size // tensor, 0)

    return (
        layer_out,
        input_grad,
        piece(0, model),
        join(qkv, 0, qw),
        join(qkv, qw, kw),
        join(qkv, qw + kw, kw),
        piece(2 * model, HEAD),
        piece(2 * model + HEAD, HEAD),
        out_wgrad,
        piece(model, model),
        join(gu, 0, fw),
        join(gu, fw, fw),
        down_wgrad,
    )


def solution(mesh):
    dp, tensor = mesh.shape["dp"], mesh.shape["tensor"]

    def run(*args):
        heads = args[4].shape[1] // HEAD // tensor
        split = 2 if dp % 2 == 0 and heads % 2 == 0 else 1
        fine = Mesh(mesh.devices.reshape(dp // split, split, tensor), ("pair", "core", "tensor"))
        token = P(("pair", "core", "tensor"), None)
        column, line, copied = P(None, "tensor"), P("tensor", None), P()
        return jax.shard_map(
            functools.partial(on_device, dp // split, split, tensor),
            mesh=fine,
            in_specs=(token, P(("pair", "core")), copied, column, column, column, copied, copied,
                      line, copied, column, column, line, token),
            out_specs=(token, token, P("tensor"), column, column, column, P("tensor"),
                       P("tensor"), line, P("tensor"), column, column, line),
            check_vma=False,
        )(*args)

    return run
```

```python
import functools
import math

import jax
import jax.numpy as jnp
from jax import lax
from jax.experimental import pallas as pl
from jax.experimental.pallas import tpu as pltpu
from jax.sharding import Mesh, PartitionSpec as P

SEQUENCE_TOKENS = 1024
HEAD = 128
epsilon = 1e-06
rope_base = 1000000.0
BF = jnp.bfloat16
F32 = jnp.float32
MIB = 1024 * 1024


def norm_forward(value, gain):
    inverse = lax.rsqrt(jnp.mean(value * value, axis=-1, keepdims=True) + epsilon)
    unit = value * inverse
    return (unit * gain, unit, inverse)


def norm_backward(grad, unit, inverse, gain):
    scaled = grad * gain
    back = inverse * (scaled - unit * jnp.mean(scaled * unit, axis=-1, keepdims=True))
    return back, grad * unit


def nn(left, right):
    return jnp.dot(left, right, preferred_element_type=F32)


def nt(left, right):
    return lax.dot_general(left, right, (((1,), (1,)), ((), ())), preferred_element_type=F32)


def tn(left, right):
    return lax.dot_general(left, right, (((0,), (0,)), ((), ())), preferred_element_type=F32)


def project(h_ref, w_ref, cos_ref, sin_ref, gq_ref, gk_ref, halo, qw):
    cos, sin = cos_ref[0], sin_ref[0]
    turn = lambda u, c, s: u * c + pltpu.roll(u, HEAD // 2, 1) * s
    kv = nn(h_ref[0], w_ref[0, :, qw:])
    kvw = kv.shape[1] // 2
    q_raw = nn(h_ref[0, halo:], w_ref[0, :, :qw])
    qs, ks = [], []
    for i in range(qw // HEAD):
        y, unit, inv = norm_forward(q_raw[:, i * HEAD : (i + 1) * HEAD], gq_ref[...])
        qs.append((turn(y, cos[halo:], sin[halo:]).astype(BF), unit, inv))
    for i in range(kvw // HEAD):
        y, unit, inv = norm_forward(kv[:, i * HEAD : (i + 1) * HEAD], gk_ref[...])
        v = kv[:, kvw + i * HEAD : kvw + (i + 1) * HEAD].astype(BF)
        ks.append((turn(y, cos, sin).astype(BF), unit, inv, v))
    return qs, ks


def attend_kernel(halo, block, qw, t_ref, h_ref, w_ref, cos_ref, sin_ref, gq_ref, gk_ref,
                  o_ref, l_ref, q_s, k_s, v_s, acc):
    qs, ks = project(h_ref, w_ref, cos_ref, sin_ref, gq_ref, gk_ref, halo, qw)
    rows = q_s.shape[0]
    group = len(qs) // len(ks)
    rate = HEAD**-0.5 * math.log2(math.e)
    whole = SEQUENCE_TOKENS // block
    first = t_ref[0] * (rows // block)
    low = lax.broadcasted_iota(jnp.int32, (block, block), 1) <= lax.broadcasted_iota(
        jnp.int32, (block, block), 0)
    for i, (q, _, _) in enumerate(qs):
        k, _, _, v = ks[i // group]
        q_s[...] = q
        if i % group == 0:
            k_s[...] = k
            v_s[...] = jnp.concatenate([v, jnp.ones_like(v)], axis=1)
        for b in range(rows // block):
            before = lax.rem(first + b, whole)
            qb = q_s[b * block : (b + 1) * block]
            own = halo + b * block
            s = nt(qb, k_s[own : own + block])
            e = jnp.where(low, jnp.exp2(s * rate), 0.0).astype(BF)
            acc[...] = nn(e, v_s[own : own + block])
            for j in range(1, whole):
                at = own - j * block
                if at < 0:
                    break

                @pl.when(before >= j)
                def _():
                    e = jnp.exp2(nt(qb, k_s[at : at + block]) * rate).astype(BF)
                    acc[...] += nn(e, v_s[at : at + block])

            inv = 1.0 / acc[:, HEAD:]
            o_ref[0, b * block : (b + 1) * block, i * HEAD : (i + 1) * HEAD] = (
                acc[:, :HEAD] * inv).astype(BF)
            l_ref[0, b * block : (b + 1) * block, i * HEAD : (i + 1) * HEAD] = inv


def attend_back_kernel(halo, block, qw, t_ref, h_ref, w_ref, cos_ref, sin_ref, gq_ref, gk_ref,
                       o_ref, l_ref, da_ref, wo_ref,
                       dq_ref, dkv_ref, share_ref, q_s, k_s, v_s, d_s, dq_s, dk_s, dv_s):
    qs, ks = project(h_ref, w_ref, cos_ref, sin_ref, gq_ref, gk_ref, halo, qw)
    rows, keys = q_s.shape[0], k_s.shape[0]
    group = len(qs) // len(ks)
    scale = HEAD**-0.5
    rate = scale * math.log2(math.e)
    whole = SEQUENCE_TOKENS // block
    first = t_ref[0] * (rows // block)
    high = lax.broadcasted_iota(jnp.int32, (block, block), 0) <= lax.broadcasted_iota(
        jnp.int32, (block, block), 1)
    cos, sin = cos_ref[0], sin_ref[0]
    back_turn = lambda g, c, s: g * c - pltpu.roll(g, HEAD // 2, 1) * s
    do = nt(da_ref[0], wo_ref[0]).astype(BF)
    kvw = len(ks) * HEAD
    share_q = jnp.zeros((1, HEAD), F32)
    share_k = jnp.zeros((1, HEAD), F32)
    for i, (q, unit_q, inv_q) in enumerate(qs):
        k, unit_k, inv_k, v = ks[i // group]
        at_head = slice(i * HEAD, (i + 1) * HEAD)
        q_s[...] = q
        if i % group == 0:
            k_s[...] = k
            lane = lax.broadcasted_iota(jnp.int32, (keys, HEAD), 1)
            v_s[...] = jnp.concatenate([v, jnp.where(lane < 2, 1.0, 0.0).astype(BF)], axis=1)
            dk_s[...] = jnp.zeros_like(dk_s)
            dv_s[...] = jnp.zeros_like(dv_s)
        d = (do[:, at_head].astype(F32) * l_ref[0, :, at_head]).astype(BF)
        delta = jnp.sum(d.astype(F32) * o_ref[0, :, at_head].astype(F32), axis=1, keepdims=True)
        upper = delta.astype(BF).astype(F32)
        lane = lax.broadcasted_iota(jnp.int32, (rows, HEAD), 1)
        extra = jnp.where(lane == 0, -upper, jnp.where(lane == 1, upper - delta, 0.0))
        d_s[...] = jnp.concatenate([d, extra.astype(BF)], axis=1)
        for b in range(rows // block):
            before = lax.rem(first + b, whole)
            qr = slice(b * block, (b + 1) * block)
            own = halo + b * block

            def part(at, masked):
                kr = slice(at, at + block)
                e = jnp.exp2(nt(k_s[kr], q_s[qr]) * rate)
                if masked:
                    e = jnp.where(high, e, 0.0)
                ds = (e * nt(v_s[kr], d_s[qr])).astype(BF)
                dv_s[kr] += nn(e.astype(BF), d_s[qr, :HEAD])
                dk_s[kr] += nn(ds, q_s[qr])
                return tn(ds, k_s[kr])

            dq_s[qr] = part(own, True)
            for j in range(1, whole):
                at = own - j * block
                if at < 0:
                    break

                @pl.when(before >= j)
                def _():
                    dq_s[qr] += part(at, False)

        grad = back_turn(dq_s[...] * scale, cos[halo:], sin[halo:])
        back, share = norm_backward(grad, unit_q, inv_q, gq_ref[...])
        share_q += jnp.sum(share, axis=0, keepdims=True)
        dq_ref[0, 0, :, at_head] = back.astype(BF)
        if i % group == group - 1:
            kh = i // group
            grad = back_turn(dk_s[...] * scale, cos, sin)
            back, share = norm_backward(grad, unit_k, inv_k, gk_ref[...])
            share_k += jnp.sum(share, axis=0, keepdims=True)
            dkv_ref[0, 0, :, kh * HEAD : (kh + 1) * HEAD] = back.astype(BF)
            dkv_ref[0, 0, :, kvw + kh * HEAD : kvw + (kh + 1) * HEAD] = dv_s[...].astype(BF)
    share_ref[0, 0] = jnp.concatenate(
        [share_q, share_k, jnp.zeros((6, HEAD), F32)], axis=0)


def attention_specs(keys, width, qkv, tensor):
    return [
        pl.BlockSpec(memory_space=pltpu.SMEM),
        pl.BlockSpec((1, keys, width), lambda s, t: (s, 0, 0)),
        pl.BlockSpec((1, width, qkv), lambda s, t: (t, 0, 0)),
        pl.BlockSpec((1, keys, HEAD), lambda s, t: (s, 0, 0)),
        pl.BlockSpec((1, keys, HEAD), lambda s, t: (s, 0, 0)),
        pl.BlockSpec((1, HEAD), lambda s, t: (0, 0)),
        pl.BlockSpec((1, HEAD), lambda s, t: (0, 0)),
    ]


def attend(block, halo, qw, t, h1, wqkv, cos, sin, gq, gk):
    split, keys, width = h1.shape
    tensor, _, qkv = wqkv.shape
    rows = keys - halo
    head_block = pl.BlockSpec((1, rows, qw), lambda s, t: (s, 0, t))
    return pl.pallas_call(
        functools.partial(attend_kernel, halo, block, qw),
        grid=(split, tensor),
        in_specs=attention_specs(keys, width, qkv, tensor),
        out_specs=[head_block, head_block],
        out_shape=[
            jax.ShapeDtypeStruct((split, rows, tensor * qw), BF),
            jax.ShapeDtypeStruct((split, rows, tensor * qw), F32),
        ],
        scratch_shapes=[
            pltpu.VMEM((rows, HEAD), BF),
            pltpu.VMEM((keys, HEAD), BF),
            pltpu.VMEM((keys, 2 * HEAD), BF),
            pltpu.VMEM((block, 2 * HEAD), F32),
        ],
        cost_estimate=pl.CostEstimate(
            flops=60_000_000_000, bytes_accessed=30_000_000, transcendentals=10_000_000),
        compiler_params=pltpu.CompilerParams(vmem_limit_bytes=48 * MIB),
    )(t, h1, wqkv, cos, sin, gq, gk)


def attend_back(block, halo, qw, t, h1, wqkv, cos, sin, gq, gk, o, l, da, wo):
    split, keys, width = h1.shape
    tensor, _, qkv = wqkv.shape
    rows = keys - halo
    head_block = pl.BlockSpec((1, rows, qw), lambda s, t: (s, 0, t))
    return pl.pallas_call(
        functools.partial(attend_back_kernel, halo, block, qw),
        grid=(split, tensor),
        in_specs=attention_specs(keys, width, qkv, tensor)
        + [
            head_block,
            head_block,
            pl.BlockSpec((1, rows, width), lambda s, t: (s, 0, 0)),
            pl.BlockSpec((1, qw, width), lambda s, t: (t, 0, 0)),
        ],
        out_specs=[
            pl.BlockSpec((1, 1, rows, qw), lambda s, t: (t, s, 0, 0)),
            pl.BlockSpec((1, 1, keys, qkv - qw), lambda s, t: (t, s, 0, 0)),
            pl.BlockSpec((1, 1, 8, HEAD), lambda s, t: (t, s, 0, 0)),
        ],
        out_shape=[
            jax.ShapeDtypeStruct((tensor, split, rows, qw), BF),
            jax.ShapeDtypeStruct((tensor, split, keys, qkv - qw), BF),
            jax.ShapeDtypeStruct((tensor, split, 8, HEAD), F32),
        ],
        scratch_shapes=[
            pltpu.VMEM((rows, HEAD), BF),
            pltpu.VMEM((keys, HEAD), BF),
            pltpu.VMEM((keys, 2 * HEAD), BF),
            pltpu.VMEM((rows, 2 * HEAD), BF),
            pltpu.VMEM((rows, HEAD), F32),
            pltpu.VMEM((keys, HEAD), F32),
            pltpu.VMEM((keys, HEAD), F32),
        ],
        cost_estimate=pl.CostEstimate(
            flops=120_000_000_000, bytes_accessed=40_000_000, transcendentals=10_000_000),
        compiler_params=pltpu.CompilerParams(vmem_limit_bytes=56 * MIB),
    )(t, h1, wqkv, cos, sin, gq, gk, o, l, da, wo)


def feed_kernel(chunk, h_ref, ht_ref, dy_ref, wgu_ref, wd_ref,
                y_ref, dh_ref, dgu_ref, dwd_ref, hid_s, dg_s, du_s):
    rows = h_ref.shape[0]
    width = wd_ref.shape[1]

    @pl.when(pl.program_id(0) == 0)
    def _():
        y_ref[...] = jnp.zeros_like(y_ref)
        dh_ref[...] = jnp.zeros_like(dh_ref)

    for c in range(rows // chunk):
        at = slice(c * chunk, (c + 1) * chunk)
        gate = nn(h_ref[at], wgu_ref[0, :, :width])
        up = nn(h_ref[at], wgu_ref[0, :, width:])
        dhid = nt(dy_ref[at], wd_ref[0])
        sigma = 1.0 / (1.0 + jnp.exp(-gate))
        act = gate * sigma
        hid_s[at] = (act * up).astype(BF)
        du_s[at] = (dhid * act).astype(BF)
        dg_s[at] = (dhid * up * (sigma + act * (1.0 - sigma))).astype(BF)
        y_ref[at] += nn(hid_s[at], wd_ref[0])
        dh_ref[at] += nt(dg_s[at], wgu_ref[0, :, :width]) + nt(du_s[at], wgu_ref[0, :, width:])
    dgu_ref[0, :, :width] = nn(ht_ref[...], dg_s[...]).astype(BF)
    dgu_ref[0, :, width:] = nn(ht_ref[...], du_s[...]).astype(BF)
    dwd_ref[0] = tn(hid_s[...], dy_ref[...]).astype(BF)


def feed(h2, dy, wgu, wd):
    rows, model = h2.shape
    tensor, _, two = wgu.shape
    width = two // 2
    whole = pl.BlockSpec(memory_space=pltpu.VMEM)
    return pl.pallas_call(
        functools.partial(feed_kernel, rows // max(1, rows // 512)),
        grid=(tensor,),
        in_specs=[
            whole, whole, whole,
            pl.BlockSpec((1, model, two), lambda t: (t, 0, 0)),
            pl.BlockSpec((1, width, model), lambda t: (t, 0, 0)),
        ],
        out_specs=[
            whole, whole,
            pl.BlockSpec((1, model, two), lambda t: (t, 0, 0)),
            pl.BlockSpec((1, width, model), lambda t: (t, 0, 0)),
        ],
        out_shape=[
            jax.ShapeDtypeStruct((rows, model), F32),
            jax.ShapeDtypeStruct((rows, model), F32),
            jax.ShapeDtypeStruct((tensor, model, two), BF),
            jax.ShapeDtypeStruct((tensor, width, model), BF),
        ],
        scratch_shapes=[pltpu.VMEM((rows, width), BF)] * 3,
        cost_estimate=pl.CostEstimate(
            flops=50_000_000_000, bytes_accessed=40_000_000, transcendentals=3_000_000),
        compiler_params=pltpu.CompilerParams(vmem_limit_bytes=58 * MIB),
    )(h2, h2.T, dy, wgu, wd)


def on_device(pairs, split, tensor, tokens, positions, first_gain, w_query, key_matrix,
              value_matrix, query_gain, key_gain, w_output, second_gain, w_gate, w_up, w_down,
              out_grad):
    rows, model = tokens.shape
    pair, core, t = lax.axis_index("pair"), lax.axis_index("core"), lax.axis_index("tensor")
    hops = max(-(-(d * rows % SEQUENCE_TOKENS) // rows) for d in range(tensor))
    halo = hops * rows
    block = math.gcd(rows, 256)
    keys = halo + rows
    spread, home = ("tensor", "pair"), ("pair", "core")

    def other(value):
        return lax.ppermute(value, "core", [(0, 1), (1, 0)])

    def both(value):
        return jnp.stack([value, other(value)]) if split == 2 else value[None]

    def own_sum(parts):
        return parts[0] + other(parts[1].astype(BF)).astype(F32) if split == 2 else parts[0]

    def columns(w):
        cols, deep = w.shape[1] // split, w.shape[0] // pairs
        return lax.dynamic_slice(w, (pair * deep, core * cols), (deep, cols))

    def lines(w):
        deep = w.shape[0] // (split * pairs)
        return lax.dynamic_slice_in_dim(w, (core * pairs + pair) * deep, deep, 0)

    def gather(w):
        return lax.all_gather(w, spread, axis=0, tiled=True)

    reach = [
        lax.ppermute(tokens, "tensor", [(d, d + h) for d in range(tensor - h)])
        for h in range(hops, 0, -1)
    ]
    wqkv = gather(jnp.concatenate([columns(w_query), columns(key_matrix), columns(value_matrix)], 1))
    wqkv = wqkv.reshape(tensor, model, -1)
    qw = w_query.shape[1] // split
    deep = model // pairs
    rest = gather(jnp.concatenate(
        [columns(w_gate), columns(w_up), lines(w_down).reshape(deep, -1),
         lines(w_output).reshape(deep, -1)], 1))
    two = 2 * (w_gate.shape[1] // split)
    wgu = rest[:, :two].reshape(tensor, model, two)
    wd = rest[:, two : two + two // 2].reshape(tensor, two // 2, model)
    wo = rest[:, two + two // 2 :].reshape(tensor, qw, model)

    gain_one = first_gain.astype(F32)
    gain_two = second_gain.astype(F32)
    gq = query_gain.astype(F32)[None]
    gk = key_gain.astype(F32)[None]
    rate = jnp.exp(-math.log(rope_base) * 2.0 * jnp.arange(HEAD // 2, dtype=F32) / HEAD)
    place = jnp.concatenate([jnp.zeros((halo,), F32), positions.astype(F32)])
    place = both(lax.dynamic_slice_in_dim(place, t * rows, keys, 0))
    angles = place[..., None] * rate
    cosine, sine = jnp.cos(angles), jnp.sin(angles)
    cos = jnp.concatenate([cosine, cosine], axis=-1)
    sin = jnp.concatenate([-sine, sine], axis=-1)
    t_ref = t[None].astype(jnp.int32)

    resid = tokens.astype(F32)
    _, unit_one, inv_one = norm_forward(resid, gain_one)
    seen = both(jnp.concatenate(reach + [tokens], axis=0))
    h1 = norm_forward(seen.astype(F32), gain_one)[0].astype(BF)
    grads = both(out_grad)
    o, l = attend(block, halo, qw, t_ref, h1, wqkv, cos, sin, gq, gk)
    o_rows = o.reshape(split * rows, -1)
    wo_flat = wo.reshape(-1, model)
    mid = resid + own_sum(nn(o_rows, wo_flat).reshape(split, rows, model))
    normed_two, unit_two, inv_two = norm_forward(mid, gain_two)
    h2 = both(normed_two.astype(BF)).reshape(split * rows, model)
    y, dh2, dgu, dwd = feed(h2, grads.reshape(split * rows, model), wgu, wd)
    layer_out = (mid + own_sum(y.reshape(split, rows, model))).astype(BF)
    dh2 = own_sum(dh2.reshape(split, rows, model))
    back_two, share_two = norm_backward(dh2, unit_two, inv_two, gain_two)
    mid_grad = out_grad.astype(F32) + back_two
    da = both(mid_grad.astype(BF))
    dwo = tn(o_rows, da.reshape(split * rows, model)).astype(BF)
    dq, dkv, shares = attend_back(
        block, halo, qw, t_ref, h1, wqkv, cos, sin, gq, gk, o, l, da, wo)

    dh_kv = jnp.zeros((split * keys, model), F32)
    dh_q = jnp.zeros((split * rows, model), F32)
    h_rows = h1[:, halo:].reshape(split * rows, model)
    h_keys = h1.reshape(split * keys, model)
    terms = []
    for d in range(tensor):
        dq_d = dq[d].reshape(split * rows, -1)
        dkv_d = dkv[d].reshape(split * keys, -1)
        dh_kv += nt(dkv_d, wqkv[d, :, qw:])
        dh_q += nt(dq_d, wqkv[d, :, :qw])
        terms.append(jnp.concatenate([tn(h_rows, dq_d), tn(h_keys, dkv_d)], axis=1).astype(BF))
    dh_kv = dh_kv.reshape(split, keys, model)
    dh_own = own_sum(dh_kv[:, halo:] + dh_q.reshape(split, rows, model))
    if hops:
        dh_far = own_sum(dh_kv[:, :halo]).astype(BF)
        for h in range(hops, 0, -1):
            at = (hops - h) * rows
            dh_own += lax.ppermute(
                dh_far[at : at + rows], "tensor", [(d + h, d) for d in range(tensor - h)]
            ).astype(F32)
    back_one, share_one = norm_backward(dh_own, unit_one, inv_one, gain_one)
    input_grad = (mid_grad + back_one).astype(BF)

    def total(wide, lined):
        cols = wide.shape[-1]
        packed = jnp.concatenate(
            [wide.reshape(-1, cols), lined.reshape(tensor * model, -1)], axis=1)
        packed = lax.psum_scatter(packed, spread, scatter_dimension=0, tiled=True)
        packed = lax.all_gather(packed, home, axis=0, tiled=True)
        packed = packed.reshape(pairs, split, deep, -1)
        lined = packed[..., cols:].transpose(1, 0, 2, 3).reshape(-1, model)
        return packed[..., :cols], lined.astype(F32)

    def join(w, start, cols):
        w = w[..., start : start + cols]
        return w.transpose(0, 2, 1, 3).reshape(model, split * cols).astype(F32)

    gu, down_wgrad = total(dgu, dwd)
    qkv, out_wgrad = total(jnp.stack(terms), dwo)
    fw = gu.shape[-1] // 2
    kw = (qkv.shape[-1] - qw) // 2
    shares = jnp.sum(shares, axis=(0, 1))
    gains = jnp.concatenate(
        [jnp.sum(share_one, axis=0), jnp.sum(share_two, axis=0), shares[0], shares[1]])
    gains = lax.psum(gains, ("pair", "core", "tensor"))

    def piece(start, size):
        return lax.dynamic_slice_in_dim(gains, start + t * (size // tensor), size // tensor, 0)

    return (
        layer_out,
        input_grad,
        piece(0, model),
        join(qkv, 0, qw),
        join(qkv, qw, kw),
        join(qkv, qw + kw, kw),
        piece(2 * model, HEAD),
        piece(2 * model + HEAD, HEAD),
        out_wgrad,
        piece(model, model),
        join(gu, 0, fw),
        join(gu, fw, fw),
        down_wgrad,
    )


def solution(mesh):
    dp, tensor = mesh.shape["dp"], mesh.shape["tensor"]

    def run(*args):
        heads = args[4].shape[1] // HEAD // tensor
        split = 2 if dp % 2 == 0 and heads % 2 == 0 else 1
        fine = Mesh(mesh.devices.reshape(dp // split, split, tensor), ("pair", "core", "tensor"))
        token = P(("pair", "core", "tensor"), None)
        column, line, copied = P(None, "tensor"), P("tensor", None), P()
        return jax.shard_map(
            functools.partial(on_device, dp // split, split, tensor),
            mesh=fine,
            in_specs=(token, P(("pair", "core")), copied, column, column, column, copied, copied,
                      line, copied, column, column, line, token),
            out_specs=(token, token, P("tensor"), column, column, column, P("tensor"),
                       P("tensor"), line, P("tensor"), column, column, line),
            check_vma=False,
        )(*args)

    return run
```
